32 devices in a mesh: group: 2 (over y), dp: 4 (over z), tensor: 4 (over x, core).
Axes of the slice: x: 2, y: 2, z: 4, core: 2. Of those that a mesh axis runs over, the one named last changes fastest.
Arguments:
- tokens: bfloat16 [4096, 4096], P(('group', 'dp', 'tensor')), parts along dimension 0, may hold values from -6 to 6
- cotangent: bfloat16 [4096, 4096], P(('group', 'dp', 'tensor')), parts along dimension 0, may hold values from -0.13183594 to 0.13183594
- weights: bfloat16 [3, 4, 262144], P(None, None, ('dp', 'tensor')), may hold values from -0.125 to 0.125
- kept: int32 [2, 4, 16], replicated, may hold values from 0 to 31, as said below
Outputs:
- weight_grads: float32 [6, 4, 262144], P('group', None, ('dp', 'tensor')), parts along dimension 0
The draws below stay inside these ranges and needn't reach their ends.
There are 2 independent parts, one for each index of `group`. The reference program is written for one: setup_inputs(seed, part) draws one part's arguments, and reference() takes and returns one part's arrays. A program takes and returns all parts, laid end to end along the dimension named above; an argument that names none is the same for every part. Nothing has to cross between parts.
Inputs may be any that keep to these rules, and one draw needn't show every extreme that they name: `kept`: each table row lists 16 distinct block indices.
All inputs are finite; a program needn't handle non-finite values.
Results may differ from the reference program's by a relative error of at most 0.0029.
Values may be sent and summed in bfloat16 or wider, within the bound.
A program may use at most 192 MiB of HBM per device.

```python
import jax
import jax.numpy as jnp
from jax import lax

D = 4096
BLK = 128
TOK_DEV = 128
KB = 32
KEEP = 16
FB = 4
TOKENS = 2048
N_DP = 4
N_TENSOR = 4


def pick_blocks(subkey):
    return jax.random.permutation(subkey, KB)[:KEEP]


def draw_kept(key, part):
    key = jax.random.fold_in(key, 7)
    subkeys = jax.random.split(key, 2 * FB)
    picked = jax.vmap(pick_blocks)(subkeys)
    return picked.reshape(2, FB, KEEP).astype(jnp.int32)


def block_levels(stream_key, extent, cuts, smallest, high):
    def one(dim, parts):
        draws = jax.random.uniform(jax.random.fold_in(jax.random.fold_in(stream_key, 6), dim), (parts,), jnp.float32, smallest / len(cuts), high / len(cuts))
        return jnp.repeat(jnp.exp(draws), extent[dim] // parts).reshape((-1,) + (1,) * (len(extent) - dim - 1))

    factor_of = one(*cuts[0])
    for cut in cuts[1:]:
        factor_of = factor_of * one(*cut)
    return factor_of


def normal_values(stream_key, dims, deviation, bound, pieces=(), kind=jnp.bfloat16):
    values = deviation * jax.random.normal(stream_key, dims, jnp.float32)
    if pieces:
        values = values * block_levels(stream_key, dims, pieces, -0.22, 0.18)
    return jnp.clip(values, -bound, bound).astype(kind)


def setup_inputs(seed: int = 0, part: int = 0) -> dict:
    key_of = jax.random.split(jax.random.key(seed), 5)
    own_keys = jax.random.split(jax.random.fold_in(key_of[4], part), 5)
    return {
        "tokens": normal_values(own_keys[0], (TOKENS, D), 1.0, 6.0, ((0, 16),)),
        "cotangent": normal_values(own_keys[1], (TOKENS, D), ((TOK_DEV * N_TENSOR * N_DP) ** -0.5), 0.13183594, ((0, 16),)),
        "weights": normal_values(key_of[2], (3, FB, KEEP * BLK * BLK), (KEEP * BLK) ** -0.5, 0.125, ((2, 16),)),
        "kept": draw_kept(jax.random.fold_in(key_of[4], 71), part),
    }


def reference(tokens, cotangent, weights, kept):
    row_count = tokens.shape[0]
    token_blocks = tokens.reshape(row_count, KB, BLK)
    cot_blocks = cotangent.reshape(row_count, KB, BLK)
    blocks = weights.reshape(3, FB, KEEP, BLK, BLK)

    def one_column(column):
        picked_x = jnp.take(token_blocks, kept[0, column], axis=1).reshape(row_count, KEEP * BLK)
        picked_y = jnp.take(cot_blocks, kept[1, column], axis=1).reshape(row_count, KEEP * BLK)
        gate_mat = blocks[0, column].reshape(KEEP * BLK, BLK)
        up_mat = blocks[1, column].reshape(KEEP * BLK, BLK)
        gate = jnp.dot(picked_x, gate_mat, preferred_element_type=jnp.float32)
        up_val = jnp.dot(picked_x, up_mat, preferred_element_type=jnp.float32)
        sigmoid_gate = jax.nn.sigmoid(gate)
        silu_gate = gate * sigmoid_gate
        hidden = (silu_gate * up_val).astype(jnp.bfloat16)
        grad_hidden = jnp.dot(picked_y,
                              jnp.transpose(blocks[2, column], (0, 2, 1)).reshape(KEEP * BLK, BLK),
                              preferred_element_type=jnp.float32)
        grad_gate = (grad_hidden * up_val * sigmoid_gate * (1.0 + gate * (1.0 - sigmoid_gate))).astype(jnp.bfloat16)
        grad_up = (grad_hidden * silu_gate).astype(jnp.bfloat16)
        gate_grad = jnp.dot(picked_x.T, grad_gate, preferred_element_type=jnp.float32)
        up_grad = jnp.dot(picked_x.T, grad_up, preferred_element_type=jnp.float32)
        down_grad = jnp.dot(hidden.T, picked_y, preferred_element_type=jnp.float32)
        down_grad = jnp.transpose(down_grad.reshape(BLK, KEEP, BLK), (1, 0, 2))
        return jnp.stack([gate_grad.reshape(-1), up_grad.reshape(-1), down_grad.reshape(-1)])

    result = lax.map(one_column, jnp.arange(FB, dtype=jnp.int32))
    return jnp.transpose(result, (1, 0, 2))
```

```python
import functools

import jax
import jax.numpy as jnp
from jax import lax
from jax.experimental import pallas as pl
from jax.experimental.pallas import tpu as pltpu
from jax.sharding import PartitionSpec as P

BLK = 128
MESH = pl.DeviceIdType.MESH
F32 = jnp.float32
BF16 = jnp.bfloat16


def activations(gate, up_val, grad_hidden):
    sigmoid_gate = jax.nn.sigmoid(gate)
    silu_gate = gate * sigmoid_gate
    hidden = (silu_gate * up_val).astype(BF16)
    grad_gate = (grad_hidden * up_val * sigmoid_gate * (1.0 + gate * (1.0 - sigmoid_gate))).astype(BF16)
    grad_up = (grad_hidden * silu_gate).astype(BF16)
    return hidden, grad_gate, grad_up


def fused_kernel(
    n_dp, n_tensor,
    kept_ref, tok_ref, cot_ref, w_ref, out_ref,
    tok_tiles, cot_tiles, pack, rows, owned, act, grads, parts,
    tok_send, tok_recv, hop_send, hop_recv, ring_send, ring_recv, grad_send, grad_recv,
):
    n_dev = n_dp * n_tensor
    keep = kept_ref.shape[2]
    tok_dev = tok_ref.shape[0]
    dp = lax.axis_index("dp")
    tensor = lax.axis_index("tensor")
    me = dp * n_tensor + tensor

    def device(index):
        return {"dp": lax.div(index, n_tensor), "tensor": lax.rem(index, n_tensor)}

    barrier = pltpu.get_barrier_semaphore()

    @pl.loop(1, n_dev)
    def _(off):
        pl.semaphore_signal(
            barrier, inc=1, device_id=device(lax.rem(me + off, n_dev)), device_id_type=MESH
        )

    pl.semaphore_wait(barrier, n_dev - 1)

    def hop(off):
        peer = lax.rem(tensor + off, n_tensor)
        return pltpu.make_async_remote_copy(
            src_ref=w_ref.at[:, peer],
            dst_ref=owned.at[:, me],
            send_sem=hop_send.at[off],
            recv_sem=hop_recv.at[tensor],
            device_id={"dp": dp, "tensor": peer},
            device_id_type=MESH,
        )

    def hop_arrival(off):
        peer = lax.rem(tensor + off, n_tensor)
        return pltpu.make_async_remote_copy(
            src_ref=w_ref.at[:, peer],
            dst_ref=owned.at[:, dp * n_tensor + peer],
            send_sem=hop_send.at[off],
            recv_sem=hop_recv.at[peer],
            device_id={"dp": dp, "tensor": peer},
            device_id_type=MESH,
        )

    for off in range(1, n_tensor):
        hop(off).start()
    for block in range(tok_tiles.shape[0]):
        tok_tiles[block] = tok_ref[:, block * BLK : (block + 1) * BLK]
        cot_tiles[block] = cot_ref[:, block * BLK : (block + 1) * BLK]
    for mat in range(3):
        owned[mat, me] = w_ref[mat, tensor]

    def pick(src_ref, table, column, dst, slot):
        for k in range(keep):
            dst[slot, table, :, k * BLK : (k + 1) * BLK] = src_ref[kept_ref[table, column, k]]

    def tok_copy(off, table):
        peer = lax.rem(tensor + off, n_tensor)
        return pltpu.make_async_remote_copy(
            src_ref=pack.at[off, table],
            dst_ref=rows.at[tensor, table],
            send_sem=tok_send.at[off, table],
            recv_sem=tok_recv.at[tensor, table],
            device_id={"dp": dp, "tensor": peer},
            device_id_type=MESH,
        )

    def tok_arrival(off, table):
        peer = lax.rem(tensor + off, n_tensor)
        return pltpu.make_async_remote_copy(
            src_ref=pack.at[off, table],
            dst_ref=rows.at[peer, table],
            send_sem=tok_send.at[off, table],
            recv_sem=tok_recv.at[peer, table],
            device_id={"dp": dp, "tensor": peer},
            device_id_type=MESH,
        )

    half = n_tensor // 2
    order = [half] + [o for o in range(1, n_tensor) if o != half]
    for off in order:
        peer = lax.rem(tensor + off, n_tensor)
        for table, src_ref in ((0, tok_tiles), (1, cot_tiles)):
            pick(src_ref, table, peer, pack, off)
            tok_copy(off, table).start()

    for off in range(1, n_tensor):
        hop_arrival(off).wait_recv()

    def ring(off, origin):
        peer = lax.rem(dp + off, n_dp)
        where = owned.at[:, pl.ds(origin * n_tensor, n_tensor)]
        return pltpu.make_async_remote_copy(
            src_ref=where,
            dst_ref=where,
            send_sem=ring_send.at[off],
            recv_sem=ring_recv.at[origin],
            device_id={"dp": peer, "tensor": tensor},
            device_id_type=MESH,
        )

    for off in range(1, n_dp):
        ring(off, dp).start()
    for table, src_ref in ((0, tok_tiles), (1, cot_tiles)):
        pick(src_ref, table, tensor, rows, tensor)
    for off in range(1, n_dp):
        ring(off, lax.rem(dp + off, n_dp)).wait_recv()

    def forward(source):
        x = rows[source, 0]
        y = rows[source, 1]
        mats = [owned[m].reshape(keep * BLK, BLK) for m in range(2)]
        gate = jnp.dot(x, mats[0], preferred_element_type=F32)
        up_val = jnp.dot(x, mats[1], preferred_element_type=F32)
        grad_hidden = jnp.zeros((tok_dev, BLK), F32)
        for k in range(keep):
            grad_hidden += lax.dot_general(
                y[:, k * BLK : (k + 1) * BLK], owned[2, k], (((1,), (1,)), ((), ())),
                preferred_element_type=F32,
            )
        hidden, grad_gate, grad_up = activations(gate, up_val, grad_hidden)
        act[source, :, 0:BLK] = grad_gate
        act[source, :, BLK : 2 * BLK] = grad_up
        act[source, :, 2 * BLK : 3 * BLK] = hidden

    @pl.loop(0, n_tensor)
    def _(off):
        @pl.when(off > 0)
        def _():
            for table in range(2):
                tok_arrival(off, table).wait_recv()

        forward(lax.rem(tensor + off, n_tensor))

    row_count = n_tensor * tok_dev

    def block_grads(index):
        lanes = pl.ds(pl.multiple_of(index * BLK, BLK), BLK)
        x = rows[:, 0, :, lanes].reshape(row_count, BLK)
        y = rows[:, 1, :, lanes].reshape(row_count, BLK)
        first = act[:, :, 0 : 2 * BLK].reshape(row_count, 2 * BLK)
        hidden = act[:, :, 2 * BLK : 3 * BLK].reshape(row_count, BLK)
        both = lax.dot_general(x, first, (((0,), (0,)), ((), ())), preferred_element_type=F32)
        down = lax.dot_general(hidden, y, (((0,), (0,)), ((), ())), preferred_element_type=F32)
        return both[:, :BLK].astype(BF16), both[:, BLK:].astype(BF16), down.astype(BF16)

    def grad_copy(index):
        return pltpu.make_async_remote_copy(
            src_ref=grads.at[index],
            dst_ref=parts.at[me],
            send_sem=grad_send.at[index],
            recv_sem=grad_recv.at[me],
            device_id=device(index),
            device_id_type=MESH,
        )

    def grad_arrival(index):
        return pltpu.make_async_remote_copy(
            src_ref=grads.at[index],
            dst_ref=parts.at[index],
            send_sem=grad_send.at[index],
            recv_sem=grad_recv.at[index],
            device_id=device(index),
            device_id_type=MESH,
        )

    def away(step):
        return lax.rem(me + 1 + lax.rem(step + n_dev // 2 - 1, n_dev - 1), n_dev)

    @pl.loop(0, n_dev - 1)
    def _(step):
        index = away(step)
        for m, block in enumerate(block_grads(index)):
            grads[index, m] = block
        grad_copy(index).start()

    for m, block in enumerate(block_grads(me)):
        parts[me, m] = block

    @pl.loop(0, n_dev - 1)
    def _(step):
        grad_arrival(away(step)).wait_recv()

    for column in range(n_tensor):
        for m in range(3):
            total = parts[column, m].astype(F32)
            for d in range(1, n_dp):
                total += parts[d * n_tensor + column, m].astype(F32)
            out_ref[m, column] = total

    for off in range(1, n_tensor):
        hop(off).wait_send()
        for table in range(2):
            tok_copy(off, table).wait_send()
    for off in range(1, n_dp):
        ring(off, dp).wait_send()

    @pl.loop(0, n_dev - 1)
    def _(step):
        grad_copy(away(step)).wait_send()


def fused(n_dp, n_tensor, tokens, cotangent, weights, kept):
    n_dev = n_dp * n_tensor
    keep = kept.shape[2]
    tok_dev = tokens.shape[0]
    vmem = pl.BlockSpec(memory_space=pltpu.VMEM)
    blocks = weights.reshape(3, n_tensor, BLK, BLK)
    out = pl.pallas_call(
        functools.partial(fused_kernel, n_dp, n_tensor),
        out_shape=jax.ShapeDtypeStruct((3, n_tensor, BLK, BLK), F32),
        in_specs=[pl.BlockSpec(memory_space=pltpu.SMEM), vmem, vmem, vmem],
        out_specs=vmem,
        scratch_shapes=[
            pltpu.VMEM((tokens.shape[1] // BLK, tok_dev, BLK), BF16),
            pltpu.VMEM((tokens.shape[1] // BLK, tok_dev, BLK), BF16),
            pltpu.VMEM((n_tensor, 2, tok_dev, keep * BLK), BF16),
            pltpu.VMEM((n_tensor, 2, tok_dev, keep * BLK), BF16),
            pltpu.VMEM((3, keep, BLK, BLK), BF16),
            pltpu.VMEM((n_tensor, tok_dev, 3 * BLK), BF16),
            pltpu.VMEM((n_dev, 3, BLK, BLK), BF16),
            pltpu.VMEM((n_dev, 3, BLK, BLK), BF16),
            pltpu.SemaphoreType.DMA((n_tensor, 2)),
            pltpu.SemaphoreType.DMA((n_tensor, 2)),
            pltpu.SemaphoreType.DMA((n_tensor,)),
            pltpu.SemaphoreType.DMA((n_tensor,)),
            pltpu.SemaphoreType.DMA((n_dp,)),
            pltpu.SemaphoreType.DMA((n_dp,)),
            pltpu.SemaphoreType.DMA((n_dev,)),
            pltpu.SemaphoreType.DMA((n_dev,)),
        ],
        compiler_params=pltpu.CompilerParams(
            collective_id=0, has_side_effects=True, vmem_limit_bytes=48 * 1024 * 1024
        ),
    )(kept, tokens, cotangent, blocks)
    return out.reshape(3, n_tensor, BLK * BLK)


def staged(tokens, cotangent, weights, kept):
    tok_rows, cot_rows = (
        lax.all_gather(tokens, "tensor", axis=0, tiled=True),
        lax.all_gather(cotangent, "tensor", axis=0, tiled=True),
    )
    tensor_size = lax.axis_size("tensor")
    dp_size = lax.axis_size("dp")
    tensor_rank = lax.axis_index("tensor")
    columns = weights.shape[1]
    cols_dev = columns // tensor_size
    slice_len = weights.shape[2]
    gathered = lax.all_gather(weights, "dp", axis=2, tiled=True)
    owned = lax.all_to_all(gathered, "tensor", split_axis=1, concat_axis=2, tiled=True)
    owned = owned.reshape(3, cols_dev, tensor_size, dp_size, slice_len)
    owned = jnp.transpose(owned, (0, 1, 3, 2, 4))
    blocks = owned.reshape(3, cols_dev, -1, BLK, BLK)
    tables = lax.dynamic_slice_in_dim(kept, tensor_rank * cols_dev, cols_dev, 1)
    row_count = tok_rows.shape[0]
    picked_x = jnp.take(tok_rows.reshape(row_count, -1, BLK), tables[0], axis=1)
    picked_y = jnp.take(cot_rows.reshape(row_count, -1, BLK), tables[1], axis=1)
    gate = jnp.einsum("rckb,ckbs->rcs", picked_x, blocks[0], preferred_element_type=F32)
    up_val = jnp.einsum("rckb,ckbs->rcs", picked_x, blocks[1], preferred_element_type=F32)
    grad_hidden = jnp.einsum("rcks,ckhs->rch", picked_y, blocks[2], preferred_element_type=F32)
    hidden, grad_gate, grad_up = activations(gate, up_val, grad_hidden)
    gate_grad = jnp.einsum("rckb,rcs->ckbs", picked_x, grad_gate, preferred_element_type=F32)
    up_grad = jnp.einsum("rckb,rcs->ckbs", picked_x, grad_up, preferred_element_type=F32)
    down_grad = jnp.einsum("rch,rcks->ckhs", hidden, picked_y, preferred_element_type=F32)
    partial_grads = jnp.stack([gate_grad, up_grad, down_grad]).reshape(3, cols_dev, -1)
    summed = lax.psum_scatter(partial_grads, "dp", scatter_dimension=2, tiled=True)
    return lax.all_to_all(summed, "tensor", split_axis=2, concat_axis=1, tiled=True)


def solution(mesh):
    n_dp, n_tensor = mesh.shape["dp"], mesh.shape["tensor"]

    def per_device(tokens, cotangent, weights, kept):
        if weights.shape[1] == n_tensor and weights.shape[2] == BLK * BLK:
            return fused(n_dp, n_tensor, tokens, cotangent, weights, kept)
        return staged(tokens, cotangent, weights, kept)

    in_specs = (
        P(("group", "dp", "tensor"), None),
        P(("group", "dp", "tensor"), None),
        P(None, None, ("dp", "tensor")),
        P(),
    )
    out_specs = P("group", None, ("dp", "tensor"))
    return jax.shard_map(
        per_device, mesh=mesh, in_specs=in_specs, out_specs=out_specs, check_vma=False
    )
```

```python
import functools

import jax
import jax.numpy as jnp
from jax import lax
from jax.experimental import pallas as pl
from jax.experimental.pallas import tpu as pltpu
from jax.sharding import PartitionSpec as P

BLK = 128
MESH = pl.DeviceIdType.MESH
F32 = jnp.float32
BF16 = jnp.bfloat16


def activations(gate, up_val, grad_hidden):
    sigmoid_gate = jax.nn.sigmoid(gate)
    silu_gate = gate * sigmoid_gate
    hidden = (silu_gate * up_val).astype(BF16)
    grad_gate = (grad_hidden * up_val * sigmoid_gate * (1.0 + gate * (1.0 - sigmoid_gate))).astype(BF16)
    grad_up = (grad_hidden * silu_gate).astype(BF16)
    return hidden, grad_gate, grad_up


def fused_kernel(
    n_dp, n_tensor,
    kept_ref, tok_ref, cot_ref, w_ref, out_ref,
    x_mine, y_mine, x_mate, y_mate, stage, owned, x_rows, x_cols, y_rows, y_blocks,
    act, hid, pair_out, pair_in, home_out, parts,
    mate_send, mate_recv, near_send, cross_send, own_recv,
    pair_send, pair_recv, home_send, home_recv,
):
    cores = 2
    cols = n_tensor // cores
    peers = n_dp * cores
    keep = kept_ref.shape[2]
    tok_dev = tok_ref.shape[0]
    dp = lax.axis_index("dp")
    tensor = lax.axis_index("tensor")
    chip = lax.div(tensor, cores)
    core = lax.rem(tensor, cores)
    far = 1 - chip
    mine = dp * cores + core
    mate = dp * cores + 1 - core

    def near(i):
        return {"dp": lax.div(i, cores), "tensor": chip * cores + lax.rem(i, cores)}

    partner = {"dp": dp, "tensor": far * cores + core}
    barrier = pltpu.get_barrier_semaphore()

    @pl.loop(1, peers)
    def _(off):
        pl.semaphore_signal(
            barrier, inc=1, device_id=near(lax.rem(mine + off, peers)), device_id_type=MESH
        )

    pl.semaphore_signal(barrier, inc=1, device_id=partner, device_id_type=MESH)

    for column in range(n_tensor):
        for m in range(3):
            stage[column, :, m * BLK : (m + 1) * BLK] = w_ref[m, column]
    for a in range(cols):
        owned[a, chip, mine] = stage[core * cols + a]

    pl.semaphore_wait(barrier, peers)

    def near_copy(a, off):
        i = lax.rem(mine + off, peers)
        return pltpu.make_async_remote_copy(
            src_ref=stage.at[lax.rem(i, cores) * cols + a],
            dst_ref=owned.at[a, chip, mine],
            send_sem=near_send.at[a, off],
            recv_sem=own_recv.at[a, chip, mine],
            device_id=near(i),
            device_id_type=MESH,
        )

    def cross_copy(a, side, i):
        return pltpu.make_async_remote_copy(
            src_ref=owned.at[a, side, i],
            dst_ref=owned.at[a, side, i],
            send_sem=cross_send.at[a, i],
            recv_sem=own_recv.at[a, side, i],
            device_id=partner,
            device_id_type=MESH,
        )

    for a in range(cols):
        cross_copy(a, chip, mine).start()
        for off in range(1, peers):
            near_copy(a, off).start()

    def mate_copy(table):
        return pltpu.make_async_remote_copy(
            src_ref=(x_mine, y_mine)[table],
            dst_ref=(x_mate, y_mate)[table],
            send_sem=mate_send.at[table],
            recv_sem=mate_recv.at[table],
            device_id=near(mate),
            device_id_type=MESH,
        )

    for table, (src_ref, tiles) in enumerate(((tok_ref, x_mine), (cot_ref, y_mine))):
        for block in range(tiles.shape[0]):
            tiles[block] = src_ref[:, block * BLK : (block + 1) * BLK]
        mate_copy(table).start()

    def relay(a, i):
        copy = cross_copy(a, chip, i)
        copy.wait_recv()
        copy.start()

    for a in range(cols):
        relay(a, mate)
    for table in range(2):
        mate_copy(table).wait_recv()

    def pack(a):
        for side in range(n_tensor // cores):
            for i in range(peers):
                k = (i // cores) * n_tensor + side * cores + i % cores
                p = side * peers + i
                lanes = slice(p * BLK, (p + 1) * BLK)
                column = core * cols + a
                index = kept_ref[0, column, k]
                block = jnp.concatenate([x_mine[index], x_mate[index]], axis=0)
                x_rows[a, :, lanes] = block
                x_cols[a, side, i] = block.T
                index = kept_ref[1, column, k]
                block = jnp.concatenate([y_mine[index], y_mate[index]], axis=0)
                y_rows[a, :, lanes] = block
                y_blocks[a, side, i] = block

    def later(step):
        return lax.rem(mine - core + cores + step, peers)

    def forward(a):
        both = jnp.dot(
            x_rows[a], owned[a, :, :, :, 0 : 2 * BLK].reshape(keep * BLK, 2 * BLK),
            preferred_element_type=F32,
        )
        grad_hidden = jnp.zeros((cores * tok_dev, BLK), F32)
        for p in range(0, keep, 2):
            side, i = divmod(p, peers)
            down = jnp.concatenate(
                [owned[a, side, i, :, 2 * BLK :], owned[a, side, i + 1, :, 2 * BLK :]], axis=1
            )
            grad_hidden += lax.dot_general(
                y_rows[a, :, p * BLK : (p + 2) * BLK], down, (((1,), (1,)), ((), ())),
                preferred_element_type=F32,
            )
        hidden, grad_gate, grad_up = activations(both[:, :BLK], both[:, BLK:], grad_hidden)
        act[a, :, 0:BLK] = grad_gate
        act[a, :, BLK : 2 * BLK] = grad_up
        hid[a] = hidden.T

    def block_grads(a, side, i):
        both = jnp.dot(x_cols[a, side, i], act[a], preferred_element_type=F32)
        down = jnp.dot(hid[a], y_blocks[a, side, i], preferred_element_type=F32)
        return jnp.concatenate([both, down], axis=1)

    def pair_copy(a, i):
        return pltpu.make_async_remote_copy(
            src_ref=pair_out.at[a, i],
            dst_ref=pair_in.at[a, i],
            send_sem=pair_send.at[a, i],
            recv_sem=pair_recv.at[a, i],
            device_id=partner,
            device_id_type=MESH,
        )

    def home_copy(a, i):
        return pltpu.make_async_remote_copy(
            src_ref=home_out.at[a, i],
            dst_ref=parts.at[core * cols + a, dp],
            send_sem=home_send.at[a, i],
            recv_sem=home_recv.at[core * cols + a, dp],
            device_id=near(i),
            device_id_type=MESH,
        )

    def to_pair(a, step):
        i = lax.rem(mine + peers // 2 + step, peers)
        pair_out[a, i] = block_grads(a, far, i).astype(BF16)
        pair_copy(a, i).start()

    def to_home(a, step):
        i = lax.rem(mine + peers // 2 + step, peers)
        pair_copy(a, i).wait_recv()
        total = (block_grads(a, chip, i) + pair_in[a, i].astype(F32)).astype(BF16)

        @pl.when(i == mine)
        def _():
            parts[core * cols + a, dp] = total

        @pl.when(i != mine)
        def _():
            home_out[a, i] = total
            home_copy(a, i).start()

    def crossed(a):
        @pl.loop(0, peers)
        def _(i):
            cross_copy(a, far, i).wait_recv()

    pack(0)

    @pl.loop(0, peers - cores)
    def _(step):
        relay(0, later(step))

    pack(1)
    crossed(0)
    forward(0)

    @pl.loop(0, peers)
    def _(step):
        @pl.when(step < peers - cores)
        def _():
            relay(1, later(step))

        to_pair(0, step)

    crossed(1)
    forward(1)

    @pl.loop(0, peers)
    def _(step):
        to_pair(1, step)
        to_home(0, step)

    @pl.loop(0, peers)
    def _(step):
        to_home(1, step)

    for column in range(n_tensor):
        for d in range(n_dp):
            @pl.when(jnp.logical_or(core != column // cols, dp != d))
            def _():
                pltpu.make_async_remote_copy(
                    src_ref=home_out.at[0, 0],
                    dst_ref=parts.at[column, d],
                    send_sem=home_send.at[0, 0],
                    recv_sem=home_recv.at[column, d],
                    device_id=near(mate),
                    device_id_type=MESH,
                ).wait_recv()

        total = parts[column, 0].astype(F32)
        for d in range(1, n_dp):
            total += parts[column, d].astype(F32)
        for m in range(3):
            out_ref[m, column] = total[:, m * BLK : (m + 1) * BLK]

    for table in range(2):
        mate_copy(table).wait_send()
    for a in range(cols):
        for off in range(1, peers):
            near_copy(a, off).wait_send()

        @pl.loop(0, peers)
        def _(i):
            cross_copy(a, chip, i).wait_send()
            pair_copy(a, i).wait_send()

            @pl.when(i != mine)
            def _():
                home_copy(a, i).wait_send()


def fused(n_dp, n_tensor, tokens, cotangent, weights, kept):
    cores, chips = 2, n_tensor // 2
    cols = n_tensor // cores
    peers = n_dp * cores
    keep = kept.shape[2]
    tok_dev = tokens.shape[0]
    tiles = tokens.shape[1] // BLK
    rows = cores * tok_dev
    vmem = pl.BlockSpec(memory_space=pltpu.VMEM)
    blocks = weights.reshape(3, n_tensor, BLK, BLK)
    dma = pltpu.SemaphoreType.DMA
    out = pl.pallas_call(
        functools.partial(fused_kernel, n_dp, n_tensor),
        out_shape=jax.ShapeDtypeStruct((3, n_tensor, BLK, BLK), F32),
        in_specs=[pl.BlockSpec(memory_space=pltpu.SMEM), vmem, vmem, vmem],
        out_specs=vmem,
        scratch_shapes=[
            pltpu.VMEM((tiles, tok_dev, BLK), BF16),
            pltpu.VMEM((tiles, tok_dev, BLK), BF16),
            pltpu.VMEM((tiles, tok_dev, BLK), BF16),
            pltpu.VMEM((tiles, tok_dev, BLK), BF16),
            pltpu.VMEM((n_tensor, BLK, 3 * BLK), BF16),
            pltpu.VMEM((cols, chips, peers, BLK, 3 * BLK), BF16),
            pltpu.VMEM((cols, rows, keep * BLK), BF16),
            pltpu.VMEM((cols, chips, peers, BLK, rows), BF16),
            pltpu.VMEM((cols, rows, keep * BLK), BF16),
            pltpu.VMEM((cols, chips, peers, rows, BLK), BF16),
            pltpu.VMEM((cols, rows, 2 * BLK), BF16),
            pltpu.VMEM((cols, BLK, rows), BF16),
            pltpu.VMEM((cols, peers, BLK, 3 * BLK), BF16),
            pltpu.VMEM((cols, peers, BLK, 3 * BLK), BF16),
            pltpu.VMEM((cols, peers, BLK, 3 * BLK), BF16),
            pltpu.VMEM((n_tensor, n_dp, BLK, 3 * BLK), BF16),
            dma((2,)),
            dma((2,)),
            dma((cols, peers)),
            dma((cols, peers)),
            dma((cols, chips, peers)),
            dma((cols, peers)),
            dma((cols, peers)),
            dma((cols, peers)),
            dma((n_tensor, n_dp)),
        ],
        compiler_params=pltpu.CompilerParams(
            collective_id=0, has_side_effects=True, vmem_limit_bytes=48 * 1024 * 1024
        ),
    )(kept, tokens, cotangent, blocks)
    return out.reshape(3, n_tensor, BLK * BLK)


def staged(tokens, cotangent, weights, kept):
    tok_rows, cot_rows = (
        lax.all_gather(tokens, "tensor", axis=0, tiled=True),
        lax.all_gather(cotangent, "tensor", axis=0, tiled=True),
    )
    tensor_size = lax.axis_size("tensor")
    dp_size = lax.axis_size("dp")
    tensor_rank = lax.axis_index("tensor")
    columns = weights.shape[1]
    cols_dev = columns // tensor_size
    slice_len = weights.shape[2]
    gathered = lax.all_gather(weights, "dp", axis=2, tiled=True)
    owned = lax.all_to_all(gathered, "tensor", split_axis=1, concat_axis=2, tiled=True)
    owned = owned.reshape(3, cols_dev, tensor_size, dp_size, slice_len)
    owned = jnp.transpose(owned, (0, 1, 3, 2, 4))
    blocks = owned.reshape(3, cols_dev, -1, BLK, BLK)
    tables = lax.dynamic_slice_in_dim(kept, tensor_rank * cols_dev, cols_dev, 1)
    row_count = tok_rows.shape[0]
    picked_x = jnp.take(tok_rows.reshape(row_count, -1, BLK), tables[0], axis=1)
    picked_y = jnp.take(cot_rows.reshape(row_count, -1, BLK), tables[1], axis=1)
    gate = jnp.einsum("rckb,ckbs->rcs", picked_x, blocks[0], preferred_element_type=F32)
    up_val = jnp.einsum("rckb,ckbs->rcs", picked_x, blocks[1], preferred_element_type=F32)
    grad_hidden = jnp.einsum("rcks,ckhs->rch", picked_y, blocks[2], preferred_element_type=F32)
    hidden, grad_gate, grad_up = activations(gate, up_val, grad_hidden)
    gate_grad = jnp.einsum("rckb,rcs->ckbs", picked_x, grad_gate, preferred_element_type=F32)
    up_grad = jnp.einsum("rckb,rcs->ckbs", picked_x, grad_up, preferred_element_type=F32)
    down_grad = jnp.einsum("rch,rcks->ckhs", hidden, picked_y, preferred_element_type=F32)
    partial_grads = jnp.stack([gate_grad, up_grad, down_grad]).reshape(3, cols_dev, -1)
    summed = lax.psum_scatter(partial_grads, "dp", scatter_dimension=2, tiled=True)
    return lax.all_to_all(summed, "tensor", split_axis=2, concat_axis=1, tiled=True)


def solution(mesh):
    n_dp, n_tensor = mesh.shape["dp"], mesh.shape["tensor"]

    def per_device(tokens, cotangent, weights, kept):
        if weights.shape[1] == n_tensor == 4 and weights.shape[2] == BLK * BLK:
            return fused(n_dp, n_tensor, tokens, cotangent, weights, kept)
        return staged(tokens, cotangent, weights, kept)

    in_specs = (
        P(("group", "dp", "tensor"), None),
        P(("group", "dp", "tensor"), None),
        P(None, None, ("dp", "tensor")),
        P(),
    )
    out_specs = P("group", None, ("dp", "tensor"))
    return jax.shard_map(
        per_device, mesh=mesh, in_specs=in_specs, out_specs=out_specs, check_vma=False
    )
```

```python
import functools

import jax
import jax.numpy as jnp
from jax import lax
from jax.experimental import pallas as pl
from jax.experimental.pallas import tpu as pltpu
from jax.sharding import PartitionSpec as P

BLK = 128
MESH = pl.DeviceIdType.MESH
F32 = jnp.float32
BF16 = jnp.bfloat16


def activations(gate, up_val, grad_hidden):
    sigmoid_gate = jax.nn.sigmoid(gate)
    silu_gate = gate * sigmoid_gate
    hidden = (silu_gate * up_val).astype(BF16)
    grad_gate = (grad_hidden * up_val * sigmoid_gate * (1.0 + gate * (1.0 - sigmoid_gate))).astype(BF16)
    grad_up = (grad_hidden * silu_gate).astype(BF16)
    return hidden, grad_gate, grad_up


def fused_kernel(
    n_dp, n_tensor,
    kept_ref, tok_ref, cot_ref, w_ref, out_ref,
    x_raw, y_raw, x_mine, y_mine, x_mate, y_mate, stage, owned, x_rows, x_cols, y_rows, y_blocks,
    act, hid, pair_out, pair_in, home_out, parts,
    fetch, mate_send, mate_recv, shard_send, line_send, cross_send, own_recv,
    pair_send, pair_recv, home_send, home_recv,
):
    cores = 2
    cols = n_tensor // cores
    peers = n_dp * cores
    keep = kept_ref.shape[2]
    tok_dev = tok_ref.shape[0]
    dp = lax.axis_index("dp")
    tensor = lax.axis_index("tensor")
    chip = lax.div(tensor, cores)
    core = lax.rem(tensor, cores)
    far = 1 - chip
    mine = dp * cores + core
    mate = dp * cores + 1 - core

    def near(i):
        return {"dp": lax.div(i, cores), "tensor": chip * cores + lax.rem(i, cores)}

    partner = {"dp": dp, "tensor": far * cores + core}
    barrier = pltpu.get_barrier_semaphore()

    def fetch_copy(table):
        return pltpu.make_async_copy(
            (tok_ref, cot_ref)[table], (x_raw, y_raw)[table], fetch.at[table]
        )

    for table in range(2):
        fetch_copy(table).start()

    @pl.loop(1, peers)
    def _(off):
        pl.semaphore_signal(
            barrier, inc=1, device_id=near(lax.rem(mine + off, peers)), device_id_type=MESH
        )

    pl.semaphore_signal(barrier, inc=1, device_id=partner, device_id_type=MESH)

    for column in range(n_tensor):
        for m in range(3):
            stage[column, :, m * BLK : (m + 1) * BLK] = w_ref[m, column]
    for a in range(cols):
        owned[a, chip, mine] = stage[core * cols + a]

    pl.semaphore_wait(barrier, peers)

    def shard_copy(a):
        return pltpu.make_async_remote_copy(
            src_ref=stage.at[(1 - core) * cols + a],
            dst_ref=owned.at[a, chip, mine],
            send_sem=shard_send.at[a],
            recv_sem=own_recv.at[a, chip, mine],
            device_id=near(mate),
            device_id_type=MESH,
        )

    def line_copy(a, way, i):
        return pltpu.make_async_remote_copy(
            src_ref=owned.at[a, chip, i],
            dst_ref=owned.at[a, chip, i],
            send_sem=line_send.at[a, way, i],
            recv_sem=own_recv.at[a, chip, i],
            device_id={"dp": dp + 2 * way - 1, "tensor": tensor},
            device_id_type=MESH,
        )

    ends = (dp > 0, dp < n_dp - 1)

    def both_ways(a, i):
        for way in range(2):
            @pl.when(ends[way])
            def _():
                line_copy(a, way, i).start()

    def cross_copy(a, side, i):
        return pltpu.make_async_remote_copy(
            src_ref=owned.at[a, side, i],
            dst_ref=owned.at[a, side, i],
            send_sem=cross_send.at[a, i],
            recv_sem=own_recv.at[a, side, i],
            device_id=partner,
            device_id_type=MESH,
        )

    for a in range(cols):
        shard_copy(a).start()
        both_ways(a, mine)
        cross_copy(a, chip, mine).start()

    def mate_copy(table):
        return pltpu.make_async_remote_copy(
            src_ref=(x_mine, y_mine)[table],
            dst_ref=(x_mate, y_mate)[table],
            send_sem=mate_send.at[table],
            recv_sem=mate_recv.at[table],
            device_id=near(mate),
            device_id_type=MESH,
        )

    for table, (src_ref, tiles) in enumerate(((x_raw, x_mine), (y_raw, y_mine))):
        fetch_copy(table).wait()
        for block in range(tiles.shape[0]):
            tiles[block] = src_ref[:, block * BLK : (block + 1) * BLK]
        mate_copy(table).start()

    for a in range(cols):
        cross_copy(a, chip, mate).wait_recv()
        both_ways(a, mate)
        cross_copy(a, chip, mate).start()

    def relay(a, step):
        hop = 1 + step // cores
        for way in range(2):
            other = dp + hop if way == 0 else dp - hop

            @pl.when((other < n_dp) if way == 0 else (other >= 0))
            def _():
                i = other * cores + lax.rem(step, cores)
                copy = cross_copy(a, chip, i)
                copy.wait_recv()

                @pl.when(ends[way])
                def _():
                    line_copy(a, way, i).start()

                copy.start()
    for table in range(2):
        mate_copy(table).wait_recv()

    def pack(a):
        for side in range(n_tensor // cores):
            for i in range(peers):
                k = (i // cores) * n_tensor + side * cores + i % cores
                p = side * peers + i
                lanes = slice(p * BLK, (p + 1) * BLK)
                column = core * cols + a
                index = kept_ref[0, column, k]
                block = jnp.concatenate([x_mine[index], x_mate[index]], axis=0)
                x_rows[a, :, lanes] = block
                x_cols[a, side, i] = block.T
                index = kept_ref[1, column, k]
                block = jnp.concatenate([y_mine[index], y_mate[index]], axis=0)
                y_rows[a, :, lanes] = block
                y_blocks[a, side, i] = block

    def forward(a):
        both = jnp.dot(
            x_rows[a], owned[a, :, :, :, 0 : 2 * BLK].reshape(keep * BLK, 2 * BLK),
            preferred_element_type=F32,
        )
        grad_hidden = jnp.zeros((cores * tok_dev, BLK), F32)
        for p in range(0, keep, 2):
            side, i = divmod(p, peers)
            down = jnp.concatenate(
                [owned[a, side, i, :, 2 * BLK :], owned[a, side, i + 1, :, 2 * BLK :]], axis=1
            )
            grad_hidden += lax.dot_general(
                y_rows[a, :, p * BLK : (p + 2) * BLK], down, (((1,), (1,)), ((), ())),
                preferred_element_type=F32,
            )
        hidden, grad_gate, grad_up = activations(both[:, :BLK], both[:, BLK:], grad_hidden)
        act[a, :, 0:BLK] = grad_gate
        act[a, :, BLK : 2 * BLK] = grad_up
        hid[a] = hidden.T

    def block_grads(a, side, i):
        both = jnp.dot(x_cols[a, side, i], act[a], preferred_element_type=F32)
        down = jnp.dot(hid[a], y_blocks[a, side, i], preferred_element_type=F32)
        return jnp.concatenate([both, down], axis=1)

    def pair_copy(a, i):
        return pltpu.make_async_remote_copy(
            src_ref=pair_out.at[a, i],
            dst_ref=pair_in.at[a, i],
            send_sem=pair_send.at[a, i],
            recv_sem=pair_recv.at[a, i],
            device_id=partner,
            device_id_type=MESH,
        )

    def home_copy(a, i):
        return pltpu.make_async_remote_copy(
            src_ref=home_out.at[a, i],
            dst_ref=parts.at[core * cols + a, dp],
            send_sem=home_send.at[a, i],
            recv_sem=home_recv.at[core * cols + a, dp],
            device_id=near(i),
            device_id_type=MESH,
        )

    def to_pair(a, step):
        i = lax.rem(mine + peers // 2 + step, peers)
        pair_out[a, i] = block_grads(a, far, i).astype(BF16)
        pair_copy(a, i).start()

    def to_home(a, step):
        i = lax.rem(mine + peers // 2 + step, peers)
        pair_copy(a, i).wait_recv()
        total = (block_grads(a, chip, i) + pair_in[a, i].astype(F32)).astype(BF16)

        @pl.when(i == mine)
        def _():
            parts[core * cols + a, dp] = total

        @pl.when(i != mine)
        def _():
            home_out[a, i] = total
            home_copy(a, i).start()

    def crossed(a):
        @pl.loop(0, peers)
        def _(i):
            cross_copy(a, far, i).wait_recv()

    pack(0)

    @pl.loop(0, peers - cores)
    def _(step):
        relay(0, step)

    pack(1)
    crossed(0)
    forward(0)

    @pl.loop(0, peers)
    def _(step):
        @pl.when(step < peers - cores)
        def _():
            relay(1, step)

        to_pair(0, step)

    crossed(1)
    forward(1)

    @pl.loop(0, peers)
    def _(step):
        to_pair(1, step)
        to_home(0, step)

    @pl.loop(0, peers)
    def _(step):
        to_home(1, step)

    for column in range(n_tensor):
        for d in range(n_dp):
            @pl.when(jnp.logical_or(core != column // cols, dp != d))
            def _():
                pltpu.make_async_remote_copy(
                    src_ref=home_out.at[0, 0],
                    dst_ref=parts.at[column, d],
                    send_sem=home_send.at[0, 0],
                    recv_sem=home_recv.at[column, d],
                    device_id=near(mate),
                    device_id_type=MESH,
                ).wait_recv()

        total = parts[column, 0].astype(F32)
        for d in range(1, n_dp):
            total += parts[column, d].astype(F32)
        for m in range(3):
            out_ref[m, column] = total[:, m * BLK : (m + 1) * BLK]

    for table in range(2):
        mate_copy(table).wait_send()
    for a in range(cols):
        shard_copy(a).wait_send()

        @pl.loop(0, peers)
        def _(i):
            cross_copy(a, chip, i).wait_send()
            pair_copy(a, i).wait_send()
            source = lax.div(i, cores)

            @pl.when(jnp.logical_and(dp > 0, source >= dp))
            def _():
                line_copy(a, 0, i).wait_send()

            @pl.when(jnp.logical_and(dp < n_dp - 1, source <= dp))
            def _():
                line_copy(a, 1, i).wait_send()

            @pl.when(i != mine)
            def _():
                home_copy(a, i).wait_send()


def fused(n_dp, n_tensor, tokens, cotangent, weights, kept):
    cores, chips = 2, n_tensor // 2
    cols = n_tensor // cores
    peers = n_dp * cores
    keep = kept.shape[2]
    tok_dev = tokens.shape[0]
    tiles = tokens.shape[1] // BLK
    rows = cores * tok_dev
    vmem = pl.BlockSpec(memory_space=pltpu.VMEM)
    hbm = pl.BlockSpec(memory_space=pl.ANY)
    blocks = weights.reshape(3, n_tensor, BLK, BLK)
    dma = pltpu.SemaphoreType.DMA
    out = pl.pallas_call(
        functools.partial(fused_kernel, n_dp, n_tensor),
        out_shape=jax.ShapeDtypeStruct((3, n_tensor, BLK, BLK), F32),
        in_specs=[pl.BlockSpec(memory_space=pltpu.SMEM), hbm, hbm, vmem],
        out_specs=vmem,
        scratch_shapes=[
            pltpu.VMEM(tokens.shape, BF16),
            pltpu.VMEM(tokens.shape, BF16),
            pltpu.VMEM((tiles, tok_dev, BLK), BF16),
            pltpu.VMEM((tiles, tok_dev, BLK), BF16),
            pltpu.VMEM((tiles, tok_dev, BLK), BF16),
            pltpu.VMEM((tiles, tok_dev, BLK), BF16),
            pltpu.VMEM((n_tensor, BLK, 3 * BLK), BF16),
            pltpu.VMEM((cols, chips, peers, BLK, 3 * BLK), BF16),
            pltpu.VMEM((cols, rows, keep * BLK), BF16),
            pltpu.VMEM((cols, chips, peers, BLK, rows), BF16),
            pltpu.VMEM((cols, rows, keep * BLK), BF16),
            pltpu.VMEM((cols, chips, peers, rows, BLK), BF16),
            pltpu.VMEM((cols, rows, 2 * BLK), BF16),
            pltpu.VMEM((cols, BLK, rows), BF16),
            pltpu.VMEM((cols, peers, BLK, 3 * BLK), BF16),
            pltpu.VMEM((cols, peers, BLK, 3 * BLK), BF16),
            pltpu.VMEM((cols, peers, BLK, 3 * BLK), BF16),
            pltpu.VMEM((n_tensor, n_dp, BLK, 3 * BLK), BF16),
            dma((2,)),
            dma((2,)),
            dma((2,)),
            dma((cols,)),
            dma((cols, 2, peers)),
            dma((cols, peers)),
            dma((cols, chips, peers)),
            dma((cols, peers)),
            dma((cols, peers)),
            dma((cols, peers)),
            dma((n_tensor, n_dp)),
        ],
        compiler_params=pltpu.CompilerParams(
            collective_id=0, has_side_effects=True, vmem_limit_bytes=48 * 1024 * 1024
        ),
    )(kept, tokens, cotangent, blocks)
    return out.reshape(3, n_tensor, BLK * BLK)


def staged(tokens, cotangent, weights, kept):
    tok_rows, cot_rows = (
        lax.all_gather(tokens, "tensor", axis=0, tiled=True),
        lax.all_gather(cotangent, "tensor", axis=0, tiled=True),
    )
    tensor_size = lax.axis_size("tensor")
    dp_size = lax.axis_size("dp")
    tensor_rank = lax.axis_index("tensor")
    columns = weights.shape[1]
    cols_dev = columns // tensor_size
    slice_len = weights.shape[2]
    gathered = lax.all_gather(weights, "dp", axis=2, tiled=True)
    owned = lax.all_to_all(gathered, "tensor", split_axis=1, concat_axis=2, tiled=True)
    owned = owned.reshape(3, cols_dev, tensor_size, dp_size, slice_len)
    owned = jnp.transpose(owned, (0, 1, 3, 2, 4))
    blocks = owned.reshape(3, cols_dev, -1, BLK, BLK)
    tables = lax.dynamic_slice_in_dim(kept, tensor_rank * cols_dev, cols_dev, 1)
    row_count = tok_rows.shape[0]
    picked_x = jnp.take(tok_rows.reshape(row_count, -1, BLK), tables[0], axis=1)
    picked_y = jnp.take(cot_rows.reshape(row_count, -1, BLK), tables[1], axis=1)
    gate = jnp.einsum("rckb,ckbs->rcs", picked_x, blocks[0], preferred_element_type=F32)
    up_val = jnp.einsum("rckb,ckbs->rcs", picked_x, blocks[1], preferred_element_type=F32)
    grad_hidden = jnp.einsum("rcks,ckhs->rch", picked_y, blocks[2], preferred_element_type=F32)
    hidden, grad_gate, grad_up = activations(gate, up_val, grad_hidden)
    gate_grad = jnp.einsum("rckb,rcs->ckbs", picked_x, grad_gate, preferred_element_type=F32)
    up_grad = jnp.einsum("rckb,rcs->ckbs", picked_x, grad_up, preferred_element_type=F32)
    down_grad = jnp.einsum("rch,rcks->ckhs", hidden, picked_y, preferred_element_type=F32)
    partial_grads = jnp.stack([gate_grad, up_grad, down_grad]).reshape(3, cols_dev, -1)
    summed = lax.psum_scatter(partial_grads, "dp", scatter_dimension=2, tiled=True)
    return lax.all_to_all(summed, "tensor", split_axis=2, concat_axis=1, tiled=True)


def solution(mesh):
    n_dp, n_tensor = mesh.shape["dp"], mesh.shape["tensor"]

    def per_device(tokens, cotangent, weights, kept):
        if weights.shape[1] == n_tensor == 4 and weights.shape[2] == BLK * BLK:
            return fused(n_dp, n_tensor, tokens, cotangent, weights, kept)
        return staged(tokens, cotangent, weights, kept)

    in_specs = (
        P(("group", "dp", "tensor"), None),
        P(("group", "dp", "tensor"), None),
        P(None, None, ("dp", "tensor")),
        P(),
    )
    out_specs = P("group", None, ("dp", "tensor"))
    return jax.shard_map(
        per_device, mesh=mesh, in_specs=in_specs, out_specs=out_specs, check_vma=False
    )
```

```python
import functools

import jax
import jax.numpy as jnp
from jax import lax
from jax.experimental import pallas as pl
from jax.experimental.pallas import tpu as pltpu
from jax.sharding import PartitionSpec as P

BLK = 128
MESH = pl.DeviceIdType.MESH
F32 = jnp.float32
BF16 = jnp.bfloat16


def activations(gate, up_val, grad_hidden):
    sigmoid_gate = jax.nn.sigmoid(gate)
    silu_gate = gate * sigmoid_gate
    hidden = (silu_gate * up_val).astype(BF16)
    grad_gate = (grad_hidden * up_val * sigmoid_gate * (1.0 + gate * (1.0 - sigmoid_gate))).astype(BF16)
    grad_up = (grad_hidden * silu_gate).astype(BF16)
    return hidden, grad_gate, grad_up


def fused_kernel(
    n_dp, n_tensor,
    kept_ref, tok_ref, cot_ref, w_ref, out_ref,
    x_raw, y_raw, x_mine, y_mine, x_mate, y_mate, stage, owned, x_rows, x_cols, y_rows, y_blocks,
    act, hid, pair_out, pair_in, home_out, parts,
    fetch, mate_send, mate_recv, shard_send, line_send, cross_send, own_recv,
    pair_send, pair_recv, home_send, home_recv,
):
    cores = 2
    cols = n_tensor // cores
    peers = n_dp * cores
    keep = kept_ref.shape[2]
    tok_dev = tok_ref.shape[0]
    dp = lax.axis_index("dp")
    tensor = lax.axis_index("tensor")
    chip = lax.div(tensor, cores)
    core = lax.rem(tensor, cores)
    far = 1 - chip
    mine = dp * cores + core
    mate = dp * cores + 1 - core

    def near(i):
        return {"dp": lax.div(i, cores), "tensor": chip * cores + lax.rem(i, cores)}

    partner = {"dp": dp, "tensor": far * cores + core}
    barrier = pltpu.get_barrier_semaphore()

    def fetch_copy(table):
        return pltpu.make_async_copy(
            (tok_ref, cot_ref)[table], (x_raw, y_raw)[table], fetch.at[table]
        )

    for table in range(2):
        fetch_copy(table).start()

    @pl.loop(1, peers)
    def _(off):
        pl.semaphore_signal(
            barrier, inc=1, device_id=near(lax.rem(mine + off, peers)), device_id_type=MESH
        )

    pl.semaphore_signal(barrier, inc=1, device_id=partner, device_id_type=MESH)

    for column in range(n_tensor):
        for m in range(3):
            stage[column, :, m * BLK : (m + 1) * BLK] = w_ref[m, column]
    for a in range(cols):
        owned[a, chip, mine] = stage[core * cols + a]

    pl.semaphore_wait(barrier, peers)

    def shard_copy(a):
        return pltpu.make_async_remote_copy(
            src_ref=stage.at[(1 - core) * cols + a],
            dst_ref=owned.at[a, chip, mine],
            send_sem=shard_send.at[a],
            recv_sem=own_recv.at[a, chip, mine],
            device_id=near(mate),
            device_id_type=MESH,
        )

    def line_copy(a, way, i):
        return pltpu.make_async_remote_copy(
            src_ref=owned.at[a, chip, i],
            dst_ref=owned.at[a, chip, i],
            send_sem=line_send.at[a, way, i],
            recv_sem=own_recv.at[a, chip, i],
            device_id={"dp": dp + 2 * way - 1, "tensor": tensor},
            device_id_type=MESH,
        )

    ends = (dp > 0, dp < n_dp - 1)

    def both_ways(a, i):
        for way in range(2):
            @pl.when(ends[way])
            def _():
                line_copy(a, way, i).start()

    def cross_copy(a, side, i):
        return pltpu.make_async_remote_copy(
            src_ref=owned.at[a, side, i],
            dst_ref=owned.at[a, side, i],
            send_sem=cross_send.at[a, i],
            recv_sem=own_recv.at[a, side, i],
            device_id=partner,
            device_id_type=MESH,
        )

    for a in range(cols):
        shard_copy(a).start()
        both_ways(a, mine)
        cross_copy(a, chip, mine).start()

    def mate_copy(table):
        return pltpu.make_async_remote_copy(
            src_ref=(x_mine, y_mine)[table],
            dst_ref=(x_mate, y_mate)[table],
            send_sem=mate_send.at[table],
            recv_sem=mate_recv.at[table],
            device_id=near(mate),
            device_id_type=MESH,
        )

    for table, (src_ref, tiles) in enumerate(((x_raw, x_mine), (y_raw, y_mine))):
        fetch_copy(table).wait()
        for block in range(tiles.shape[0]):
            tiles[block] = src_ref[:, block * BLK : (block + 1) * BLK]
        mate_copy(table).start()

    for a in range(cols):
        cross_copy(a, chip, mate).wait_recv()
        both_ways(a, mate)
        cross_copy(a, chip, mate).start()

    def relay(a, step):
        hop = 1 + step // cores
        for way in range(2):
            other = dp + hop if way == 0 else dp - hop

            @pl.when((other < n_dp) if way == 0 else (other >= 0))
            def _():
                i = other * cores + lax.rem(step, cores)
                copy = cross_copy(a, chip, i)
                copy.wait_recv()

                @pl.when(ends[way])
                def _():
                    line_copy(a, way, i).start()

                copy.start()
    for table in range(2):
        mate_copy(table).wait_recv()

    def pack(a):
        for side in range(n_tensor // cores):
            for i in range(peers):
                k = (i // cores) * n_tensor + side * cores + i % cores
                p = side * peers + i
                lanes = slice(p * BLK, (p + 1) * BLK)
                column = core * cols + a
                index = kept_ref[0, column, k]
                block = jnp.concatenate([x_mine[index], x_mate[index]], axis=0)
                x_rows[a, :, lanes] = block
                x_cols[a, side, i] = block.T
                index = kept_ref[1, column, k]
                block = jnp.concatenate([y_mine[index], y_mate[index]], axis=0)
                y_rows[a, :, lanes] = block
                y_blocks[a, side, i] = block

    def forward(a):
        both = jnp.dot(
            x_rows[a], owned[a, :, :, :, 0 : 2 * BLK].reshape(keep * BLK, 2 * BLK),
            preferred_element_type=F32,
        )
        grad_hidden = jnp.zeros((cores * tok_dev, BLK), F32)
        for p in range(0, keep, 2):
            side, i = divmod(p, peers)
            down = jnp.concatenate(
                [owned[a, side, i, :, 2 * BLK :], owned[a, side, i + 1, :, 2 * BLK :]], axis=1
            )
            grad_hidden += lax.dot_general(
                y_rows[a, :, p * BLK : (p + 2) * BLK], down, (((1,), (1,)), ((), ())),
                preferred_element_type=F32,
            )
        hidden, grad_gate, grad_up = activations(both[:, :BLK], both[:, BLK:], grad_hidden)
        act[a, :, 0:BLK] = grad_gate
        act[a, :, BLK : 2 * BLK] = grad_up
        hid[a] = hidden.T

    def block_grads(a, side, i):
        both = jnp.dot(x_cols[a, side, i], act[a], preferred_element_type=F32)
        down = jnp.dot(hid[a], y_blocks[a, side, i], preferred_element_type=F32)
        return jnp.concatenate([both, down], axis=1)

    def pair_copy(a, i):
        return pltpu.make_async_remote_copy(
            src_ref=pair_out.at[a, i],
            dst_ref=pair_in.at[a, i],
            send_sem=pair_send.at[a, i],
            recv_sem=pair_recv.at[a, i],
            device_id=partner,
            device_id_type=MESH,
        )

    def home_copy(a, i):
        return pltpu.make_async_remote_copy(
            src_ref=home_out.at[a, i],
            dst_ref=parts.at[core * cols + a, dp],
            send_sem=home_send.at[a, i],
            recv_sem=home_recv.at[core * cols + a, dp],
            device_id=near(i),
            device_id_type=MESH,
        )

    def to_pair(a, step):
        i = lax.rem(mine + peers // 2 + step, peers)
        pair_out[a, i] = block_grads(a, far, i).astype(BF16)
        pair_copy(a, i).start()

    def to_home(a, step):
        i = lax.rem(mine + peers // 2 + step, peers)
        pair_copy(a, i).wait_recv()
        total = (block_grads(a, chip, i) + pair_in[a, i].astype(F32)).astype(BF16)

        @pl.when(i == mine)
        def _():
            parts[core * cols + a, dp] = total

        @pl.when(i != mine)
        def _():
            home_out[a, i] = total
            home_copy(a, i).start()

    def crossed(a):
        @pl.loop(0, peers)
        def _(i):
            cross_copy(a, far, i).wait_recv()

    pack(0)

    @pl.loop(0, peers - cores)
    def _(step):
        relay(0, step)

    pack(1)

    @pl.loop(0, peers - cores)
    def _(step):
        relay(1, step)

    crossed(0)
    forward(0)

    @pl.loop(0, peers)
    def _(step):
        to_pair(0, step)

    crossed(1)
    forward(1)

    @pl.loop(0, peers)
    def _(step):
        to_pair(1, step)
        to_home(0, step)

    @pl.loop(0, peers)
    def _(step):
        to_home(1, step)

    for column in range(n_tensor):
        for d in range(n_dp):
            @pl.when(jnp.logical_or(core != column // cols, dp != d))
            def _():
                pltpu.make_async_remote_copy(
                    src_ref=home_out.at[0, 0],
                    dst_ref=parts.at[column, d],
                    send_sem=home_send.at[0, 0],
                    recv_sem=home_recv.at[column, d],
                    device_id=near(mate),
                    device_id_type=MESH,
                ).wait_recv()

        total = parts[column, 0].astype(F32)
        for d in range(1, n_dp):
            total += parts[column, d].astype(F32)
        for m in range(3):
            out_ref[m, column] = total[:, m * BLK : (m + 1) * BLK]

    for table in range(2):
        mate_copy(table).wait_send()
    for a in range(cols):
        shard_copy(a).wait_send()

        @pl.loop(0, peers)
        def _(i):
            cross_copy(a, chip, i).wait_send()
            pair_copy(a, i).wait_send()
            source = lax.div(i, cores)

            @pl.when(jnp.logical_and(dp > 0, source >= dp))
            def _():
                line_copy(a, 0, i).wait_send()

            @pl.when(jnp.logical_and(dp < n_dp - 1, source <= dp))
            def _():
                line_copy(a, 1, i).wait_send()

            @pl.when(i != mine)
            def _():
                home_copy(a, i).wait_send()


def fused(n_dp, n_tensor, tokens, cotangent, weights, kept):
    cores, chips = 2, n_tensor // 2
    cols = n_tensor // cores
    peers = n_dp * cores
    keep = kept.shape[2]
    tok_dev = tokens.shape[0]
    tiles = tokens.shape[1] // BLK
    rows = cores * tok_dev
    vmem = pl.BlockSpec(memory_space=pltpu.VMEM)
    hbm = pl.BlockSpec(memory_space=pl.ANY)
    blocks = weights.reshape(3, n_tensor, BLK, BLK)
    dma = pltpu.SemaphoreType.DMA
    out = pl.pallas_call(
        functools.partial(fused_kernel, n_dp, n_tensor),
        out_shape=jax.ShapeDtypeStruct((3, n_tensor, BLK, BLK), F32),
        in_specs=[pl.BlockSpec(memory_space=pltpu.SMEM), hbm, hbm, vmem],
        out_specs=vmem,
        scratch_shapes=[
            pltpu.VMEM(tokens.shape, BF16),
            pltpu.VMEM(tokens.shape, BF16),
            pltpu.VMEM((tiles, tok_dev, BLK), BF16),
            pltpu.VMEM((tiles, tok_dev, BLK), BF16),
            pltpu.VMEM((tiles, tok_dev, BLK), BF16),
            pltpu.VMEM((tiles, tok_dev, BLK), BF16),
            pltpu.VMEM((n_tensor, BLK, 3 * BLK), BF16),
            pltpu.VMEM((cols, chips, peers, BLK, 3 * BLK), BF16),
            pltpu.VMEM((cols, rows, keep * BLK), BF16),
            pltpu.VMEM((cols, chips, peers, BLK, rows), BF16),
            pltpu.VMEM((cols, rows, keep * BLK), BF16),
            pltpu.VMEM((cols, chips, peers, rows, BLK), BF16),
            pltpu.VMEM((cols, rows, 2 * BLK), BF16),
            pltpu.VMEM((cols, BLK, rows), BF16),
            pltpu.VMEM((cols, peers, BLK, 3 * BLK), BF16),
            pltpu.VMEM((cols, peers, BLK, 3 * BLK), BF16),
            pltpu.VMEM((cols, peers, BLK, 3 * BLK), BF16),
            pltpu.VMEM((n_tensor, n_dp, BLK, 3 * BLK), BF16),
            dma((2,)),
            dma((2,)),
            dma((2,)),
            dma((cols,)),
            dma((cols, 2, peers)),
            dma((cols, peers)),
            dma((cols, chips, peers)),
            dma((cols, peers)),
            dma((cols, peers)),
            dma((cols, peers)),
            dma((n_tensor, n_dp)),
        ],
        compiler_params=pltpu.CompilerParams(
            collective_id=0, has_side_effects=True, vmem_limit_bytes=48 * 1024 * 1024
        ),
    )(kept, tokens, cotangent, blocks)
    return out.reshape(3, n_tensor, BLK * BLK)


def staged(tokens, cotangent, weights, kept):
    tok_rows, cot_rows = (
        lax.all_gather(tokens, "tensor", axis=0, tiled=True),
        lax.all_gather(cotangent, "tensor", axis=0, tiled=True),
    )
    tensor_size = lax.axis_size("tensor")
    dp_size = lax.axis_size("dp")
    tensor_rank = lax.axis_index("tensor")
    columns = weights.shape[1]
    cols_dev = columns // tensor_size
    slice_len = weights.shape[2]
    gathered = lax.all_gather(weights, "dp", axis=2, tiled=True)
    owned = lax.all_to_all(gathered, "tensor", split_axis=1, concat_axis=2, tiled=True)
    owned = owned.reshape(3, cols_dev, tensor_size, dp_size, slice_len)
    owned = jnp.transpose(owned, (0, 1, 3, 2, 4))
    blocks = owned.reshape(3, cols_dev, -1, BLK, BLK)
    tables = lax.dynamic_slice_in_dim(kept, tensor_rank * cols_dev, cols_dev, 1)
    row_count = tok_rows.shape[0]
    picked_x = jnp.take(tok_rows.reshape(row_count, -1, BLK), tables[0], axis=1)
    picked_y = jnp.take(cot_rows.reshape(row_count, -1, BLK), tables[1], axis=1)
    gate = jnp.einsum("rckb,ckbs->rcs", picked_x, blocks[0], preferred_element_type=F32)
    up_val = jnp.einsum("rckb,ckbs->rcs", picked_x, blocks[1], preferred_element_type=F32)
    grad_hidden = jnp.einsum("rcks,ckhs->rch", picked_y, blocks[2], preferred_element_type=F32)
    hidden, grad_gate, grad_up = activations(gate, up_val, grad_hidden)
    gate_grad = jnp.einsum("rckb,rcs->ckbs", picked_x, grad_gate, preferred_element_type=F32)
    up_grad = jnp.einsum("rckb,rcs->ckbs", picked_x, grad_up, preferred_element_type=F32)
    down_grad = jnp.einsum("rch,rcks->ckhs", hidden, picked_y, preferred_element_type=F32)
    partial_grads = jnp.stack([gate_grad, up_grad, down_grad]).reshape(3, cols_dev, -1)
    summed = lax.psum_scatter(partial_grads, "dp", scatter_dimension=2, tiled=True)
    return lax.all_to_all(summed, "tensor", split_axis=2, concat_axis=1, tiled=True)


def solution(mesh):
    n_dp, n_tensor = mesh.shape["dp"], mesh.shape["tensor"]

    def per_device(tokens, cotangent, weights, kept):
        if weights.shape[1] == n_tensor == 4 and weights.shape[2] == BLK * BLK:
            return fused(n_dp, n_tensor, tokens, cotangent, weights, kept)
        return staged(tokens, cotangent, weights, kept)

    in_specs = (
        P(("group", "dp", "tensor"), None),
        P(("group", "dp", "tensor"), None),
        P(None, None, ("dp", "tensor")),
        P(),
    )
    out_specs = P("group", None, ("dp", "tensor"))
    return jax.shard_map(
        per_device, mesh=mesh, in_specs=in_specs, out_specs=out_specs, check_vma=False
    )
```

```python
import functools

import jax
import jax.numpy as jnp
from jax import lax
from jax.experimental import pallas as pl
from jax.experimental.pallas import tpu as pltpu
from jax.sharding import PartitionSpec as P

BLK = 128
MESH = pl.DeviceIdType.MESH
F32 = jnp.float32
BF16 = jnp.bfloat16


def activations(gate, up_val, grad_hidden):
    sigmoid_gate = jax.nn.sigmoid(gate)
    silu_gate = gate * sigmoid_gate
    hidden = (silu_gate * up_val).astype(BF16)
    grad_gate = (grad_hidden * up_val * sigmoid_gate * (1.0 + gate * (1.0 - sigmoid_gate))).astype(BF16)
    grad_up = (grad_hidden * silu_gate).astype(BF16)
    return hidden, grad_gate, grad_up


def fused_kernel(
    n_dp, n_tensor,
    kept_ref, tok_ref, cot_ref, w_ref, out_ref,
    x_raw, y_raw, x_mine, y_mine, x_mate, y_mate, stage, owned, x_rows, x_cols, y_rows, y_blocks,
    act, hid, pair_out, pair_in, home_out, parts,
    fetch, mate_send, mate_recv, shard_send, line_send, cross_send, own_recv,
    pair_send, pair_recv, home_send, home_recv,
):
    cores = 2
    cols = n_tensor // cores
    peers = n_dp * cores
    keep = kept_ref.shape[2]
    tok_dev = tok_ref.shape[0]
    dp = lax.axis_index("dp")
    tensor = lax.axis_index("tensor")
    chip = lax.div(tensor, cores)
    core = lax.rem(tensor, cores)
    far = 1 - chip
    mine = dp * cores + core
    mate = dp * cores + 1 - core

    def near(i):
        return {"dp": lax.div(i, cores), "tensor": chip * cores + lax.rem(i, cores)}

    partner = {"dp": dp, "tensor": far * cores + core}
    barrier = pltpu.get_barrier_semaphore()

    def fetch_copy(table):
        return pltpu.make_async_copy(
            (tok_ref, cot_ref)[table], (x_raw, y_raw)[table], fetch.at[table]
        )

    for table in range(2):
        fetch_copy(table).start()

    @pl.loop(1, peers)
    def _(off):
        pl.semaphore_signal(
            barrier, inc=1, device_id=near(lax.rem(mine + off, peers)), device_id_type=MESH
        )

    pl.semaphore_signal(barrier, inc=1, device_id=partner, device_id_type=MESH)

    for column in range(n_tensor):
        for m in range(3):
            stage[column, :, m * BLK : (m + 1) * BLK] = w_ref[m, column]
    for a in range(cols):
        owned[a, chip, mine] = stage[core * cols + a]

    pl.semaphore_wait(barrier, peers)

    def shard_copy(a):
        return pltpu.make_async_remote_copy(
            src_ref=stage.at[(1 - core) * cols + a],
            dst_ref=owned.at[a, chip, mine],
            send_sem=shard_send.at[a],
            recv_sem=own_recv.at[a, chip, mine],
            device_id=near(mate),
            device_id_type=MESH,
        )

    def line_copy(a, way, i):
        return pltpu.make_async_remote_copy(
            src_ref=owned.at[a, chip, i],
            dst_ref=owned.at[a, chip, i],
            send_sem=line_send.at[a, way, i],
            recv_sem=own_recv.at[a, chip, i],
            device_id={"dp": dp + 2 * way - 1, "tensor": tensor},
            device_id_type=MESH,
        )

    ends = (dp > 0, dp < n_dp - 1)

    def both_ways(a, i):
        for way in range(2):
            @pl.when(ends[way])
            def _():
                line_copy(a, way, i).start()

    def cross_copy(a, side, i):
        return pltpu.make_async_remote_copy(
            src_ref=owned.at[a, side, i],
            dst_ref=owned.at[a, side, i],
            send_sem=cross_send.at[a, i],
            recv_sem=own_recv.at[a, side, i],
            device_id=partner,
            device_id_type=MESH,
        )

    for a in range(cols):
        shard_copy(a).start()
        both_ways(a, mine)
        cross_copy(a, chip, mine).start()

    for a in range(cols):
        cross_copy(a, chip, mate).wait_recv()
        both_ways(a, mate)
        cross_copy(a, chip, mate).start()

    def mate_copy(table):
        return pltpu.make_async_remote_copy(
            src_ref=(x_mine, y_mine)[table],
            dst_ref=(x_mate, y_mate)[table],
            send_sem=mate_send.at[table],
            recv_sem=mate_recv.at[table],
            device_id=near(mate),
            device_id_type=MESH,
        )

    for table, (src_ref, tiles) in enumerate(((x_raw, x_mine), (y_raw, y_mine))):
        fetch_copy(table).wait()
        for block in range(tiles.shape[0]):
            tiles[block] = src_ref[:, block * BLK : (block + 1) * BLK]
        mate_copy(table).start()

    def relay(a, step):
        hop = 1 + step // cores
        for way in range(2):
            other = dp + hop if way == 0 else dp - hop

            @pl.when((other < n_dp) if way == 0 else (other >= 0))
            def _():
                i = other * cores + lax.rem(step, cores)
                copy = cross_copy(a, chip, i)
                copy.wait_recv()

                @pl.when(ends[way])
                def _():
                    line_copy(a, way, i).start()

                copy.start()
    for table in range(2):
        mate_copy(table).wait_recv()

    def pack(a):
        for side in range(n_tensor // cores):
            for i in range(peers):
                k = (i // cores) * n_tensor + side * cores + i % cores
                p = side * peers + i
                lanes = slice(p * BLK, (p + 1) * BLK)
                column = core * cols + a
                index = kept_ref[0, column, k]
                block = jnp.concatenate([x_mine[index], x_mate[index]], axis=0)
                x_rows[a, :, lanes] = block
                x_cols[a, side, i] = block.T
                index = kept_ref[1, column, k]
                block = jnp.concatenate([y_mine[index], y_mate[index]], axis=0)
                y_rows[a, :, lanes] = block
                y_blocks[a, side, i] = block

    def forward(a):
        both = jnp.dot(
            x_rows[a], owned[a, :, :, :, 0 : 2 * BLK].reshape(keep * BLK, 2 * BLK),
            preferred_element_type=F32,
        )
        grad_hidden = jnp.zeros((cores * tok_dev, BLK), F32)
        for p in range(0, keep, 2):
            side, i = divmod(p, peers)
            down = jnp.concatenate(
                [owned[a, side, i, :, 2 * BLK :], owned[a, side, i + 1, :, 2 * BLK :]], axis=1
            )
            grad_hidden += lax.dot_general(
                y_rows[a, :, p * BLK : (p + 2) * BLK], down, (((1,), (1,)), ((), ())),
                preferred_element_type=F32,
            )
        hidden, grad_gate, grad_up = activations(both[:, :BLK], both[:, BLK:], grad_hidden)
        act[a, :, 0:BLK] = grad_gate
        act[a, :, BLK : 2 * BLK] = grad_up
        hid[a] = hidden.T

    def block_grads(a, side, i):
        both = jnp.dot(x_cols[a, side, i], act[a], preferred_element_type=F32)
        down = jnp.dot(hid[a], y_blocks[a, side, i], preferred_element_type=F32)
        return jnp.concatenate([both, down], axis=1)

    def pair_copy(a, i):
        return pltpu.make_async_remote_copy(
            src_ref=pair_out.at[a, i],
            dst_ref=pair_in.at[a, i],
            send_sem=pair_send.at[a, i],
            recv_sem=pair_recv.at[a, i],
            device_id=partner,
            device_id_type=MESH,
        )

    def home_copy(a, i):
        return pltpu.make_async_remote_copy(
            src_ref=home_out.at[a, i],
            dst_ref=parts.at[core * cols + a, dp],
            send_sem=home_send.at[a, i],
            recv_sem=home_recv.at[core * cols + a, dp],
            device_id=near(i),
            device_id_type=MESH,
        )

    def to_pair(a, step):
        i = lax.rem(mine + peers // 2 + step, peers)
        pair_out[a, i] = block_grads(a, far, i).astype(BF16)
        pair_copy(a, i).start()

    def to_home(a, step):
        i = lax.rem(mine + peers // 2 + step, peers)
        pair_copy(a, i).wait_recv()
        total = (block_grads(a, chip, i) + pair_in[a, i].astype(F32)).astype(BF16)

        @pl.when(i == mine)
        def _():
            parts[core * cols + a, dp] = total

        @pl.when(i != mine)
        def _():
            home_out[a, i] = total
            home_copy(a, i).start()

    def crossed(a):
        @pl.loop(0, peers)
        def _(i):
            cross_copy(a, far, i).wait_recv()

    pack(0)

    @pl.loop(0, peers - cores)
    def _(step):
        relay(0, step)

    @pl.loop(0, peers - cores)
    def _(step):
        relay(1, step)

    crossed(0)
    forward(0)

    @pl.loop(0, peers)
    def _(step):
        to_pair(0, step)

    pack(1)
    crossed(1)
    forward(1)

    @pl.loop(0, peers)
    def _(step):
        to_pair(1, step)
        to_home(0, step)

    @pl.loop(0, peers)
    def _(step):
        to_home(1, step)

    for column in range(n_tensor):
        for d in range(n_dp):
            @pl.when(jnp.logical_or(core != column // cols, dp != d))
            def _():
                pltpu.make_async_remote_copy(
                    src_ref=home_out.at[0, 0],
                    dst_ref=parts.at[column, d],
                    send_sem=home_send.at[0, 0],
                    recv_sem=home_recv.at[column, d],
                    device_id=near(mate),
                    device_id_type=MESH,
                ).wait_recv()

        total = parts[column, 0].astype(F32)
        for d in range(1, n_dp):
            total += parts[column, d].astype(F32)
        for m in range(3):
            out_ref[m, column] = total[:, m * BLK : (m + 1) * BLK]

    for table in range(2):
        mate_copy(table).wait_send()
    for a in range(cols):
        shard_copy(a).wait_send()

        @pl.loop(0, peers)
        def _(i):
            cross_copy(a, chip, i).wait_send()
            pair_copy(a, i).wait_send()
            source = lax.div(i, cores)

            @pl.when(jnp.logical_and(dp > 0, source >= dp))
            def _():
                line_copy(a, 0, i).wait_send()

            @pl.when(jnp.logical_and(dp < n_dp - 1, source <= dp))
            def _():
                line_copy(a, 1, i).wait_send()

            @pl.when(i != mine)
            def _():
                home_copy(a, i).wait_send()


def fused(n_dp, n_tensor, tokens, cotangent, weights, kept):
    cores, chips = 2, n_tensor // 2
    cols = n_tensor // cores
    peers = n_dp * cores
    keep = kept.shape[2]
    tok_dev = tokens.shape[0]
    tiles = tokens.shape[1] // BLK
    rows = cores * tok_dev
    vmem = pl.BlockSpec(memory_space=pltpu.VMEM)
    hbm = pl.BlockSpec(memory_space=pl.ANY)
    blocks = weights.reshape(3, n_tensor, BLK, BLK)
    dma = pltpu.SemaphoreType.DMA
    out = pl.pallas_call(
        functools.partial(fused_kernel, n_dp, n_tensor),
        out_shape=jax.ShapeDtypeStruct((3, n_tensor, BLK, BLK), F32),
        in_specs=[pl.BlockSpec(memory_space=pltpu.SMEM), hbm, hbm, vmem],
        out_specs=vmem,
        scratch_shapes=[
            pltpu.VMEM(tokens.shape, BF16),
            pltpu.VMEM(tokens.shape, BF16),
            pltpu.VMEM((tiles, tok_dev, BLK), BF16),
            pltpu.VMEM((tiles, tok_dev, BLK), BF16),
            pltpu.VMEM((tiles, tok_dev, BLK), BF16),
            pltpu.VMEM((tiles, tok_dev, BLK), BF16),
            pltpu.VMEM((n_tensor, BLK, 3 * BLK), BF16),
            pltpu.VMEM((cols, chips, peers, BLK, 3 * BLK), BF16),
            pltpu.VMEM((cols, rows, keep * BLK), BF16),
            pltpu.VMEM((cols, chips, peers, BLK, rows), BF16),
            pltpu.VMEM((cols, rows, keep * BLK), BF16),
            pltpu.VMEM((cols, chips, peers, rows, BLK), BF16),
            pltpu.VMEM((cols, rows, 2 * BLK), BF16),
            pltpu.VMEM((cols, BLK, rows), BF16),
            pltpu.VMEM((cols, peers, BLK, 3 * BLK), BF16),
            pltpu.VMEM((cols, peers, BLK, 3 * BLK), BF16),
            pltpu.VMEM((cols, peers, BLK, 3 * BLK), BF16),
            pltpu.VMEM((n_tensor, n_dp, BLK, 3 * BLK), BF16),
            dma((2,)),
            dma((2,)),
            dma((2,)),
            dma((cols,)),
            dma((cols, 2, peers)),
            dma((cols, peers)),
            dma((cols, chips, peers)),
            dma((cols, peers)),
            dma((cols, peers)),
            dma((cols, peers)),
            dma((n_tensor, n_dp)),
        ],
        compiler_params=pltpu.CompilerParams(
            collective_id=0, has_side_effects=True, vmem_limit_bytes=48 * 1024 * 1024
        ),
    )(kept, tokens, cotangent, blocks)
    return out.reshape(3, n_tensor, BLK * BLK)


def staged(tokens, cotangent, weights, kept):
    tok_rows, cot_rows = (
        lax.all_gather(tokens, "tensor", axis=0, tiled=True),
        lax.all_gather(cotangent, "tensor", axis=0, tiled=True),
    )
    tensor_size = lax.axis_size("tensor")
    dp_size = lax.axis_size("dp")
    tensor_rank = lax.axis_index("tensor")
    columns = weights.shape[1]
    cols_dev = columns // tensor_size
    slice_len = weights.shape[2]
    gathered = lax.all_gather(weights, "dp", axis=2, tiled=True)
    owned = lax.all_to_all(gathered, "tensor", split_axis=1, concat_axis=2, tiled=True)
    owned = owned.reshape(3, cols_dev, tensor_size, dp_size, slice_len)
    owned = jnp.transpose(owned, (0, 1, 3, 2, 4))
    blocks = owned.reshape(3, cols_dev, -1, BLK, BLK)
    tables = lax.dynamic_slice_in_dim(kept, tensor_rank * cols_dev, cols_dev, 1)
    row_count = tok_rows.shape[0]
    picked_x = jnp.take(tok_rows.reshape(row_count, -1, BLK), tables[0], axis=1)
    picked_y = jnp.take(cot_rows.reshape(row_count, -1, BLK), tables[1], axis=1)
    gate = jnp.einsum("rckb,ckbs->rcs", picked_x, blocks[0], preferred_element_type=F32)
    up_val = jnp.einsum("rckb,ckbs->rcs", picked_x, blocks[1], preferred_element_type=F32)
    grad_hidden = jnp.einsum("rcks,ckhs->rch", picked_y, blocks[2], preferred_element_type=F32)
    hidden, grad_gate, grad_up = activations(gate, up_val, grad_hidden)
    gate_grad = jnp.einsum("rckb,rcs->ckbs", picked_x, grad_gate, preferred_element_type=F32)
    up_grad = jnp.einsum("rckb,rcs->ckbs", picked_x, grad_up, preferred_element_type=F32)
    down_grad = jnp.einsum("rch,rcks->ckhs", hidden, picked_y, preferred_element_type=F32)
    partial_grads = jnp.stack([gate_grad, up_grad, down_grad]).reshape(3, cols_dev, -1)
    summed = lax.psum_scatter(partial_grads, "dp", scatter_dimension=2, tiled=True)
    return lax.all_to_all(summed, "tensor", split_axis=2, concat_axis=1, tiled=True)


def solution(mesh):
    n_dp, n_tensor = mesh.shape["dp"], mesh.shape["tensor"]

    def per_device(tokens, cotangent, weights, kept):
        if weights.shape[1] == n_tensor == 4 and weights.shape[2] == BLK * BLK:
            return fused(n_dp, n_tensor, tokens, cotangent, weights, kept)
        return staged(tokens, cotangent, weights, kept)

    in_specs = (
        P(("group", "dp", "tensor"), None),
        P(("group", "dp", "tensor"), None),
        P(None, None, ("dp", "tensor")),
        P(),
    )
    out_specs = P("group", None, ("dp", "tensor"))
    return jax.shard_map(
        per_device, mesh=mesh, in_specs=in_specs, out_specs=out_specs, check_vma=False
    )
```
